256 devices in a mesh: dp: 16 (over z, core), seq: 16 (over y, x).
Axes of the slice: x: 4, y: 4, z: 8, core: 2. Of those that a mesh axis runs over, the one named last changes fastest.
Arguments:
- queries: bfloat16 [16, 4096, 1024], P('dp', 'seq'), may hold values from -80 to 80
- keys: bfloat16 [16, 4096, 1024], P('dp', 'seq'), may hold values from -80 to 80
- values: bfloat16 [16, 4096, 1024], P('dp', 'seq'), may hold values from -12 to 12
- upstream: bfloat16 [16, 4096, 1024], P('dp', 'seq'), may hold values from -6 to 6
- w_out: bfloat16 [1024, 1024], replicated, may hold values from -0.1875 to 0.1875
- key_blocks: int32 [16, 32, 16], P('dp'), may hold values from 0 to 31, as said below
- block_counts: int32 [16, 32], P('dp'), may hold values from 1 to 16, as said below
Outputs:
- mixed: bfloat16 [16, 4096, 1024], P('dp', 'seq')
- grad_q: bfloat16 [16, 4096, 1024], P('dp', 'seq')
- grad_k: bfloat16 [16, 4096, 1024], P('dp', 'seq')
- grad_v: bfloat16 [16, 4096, 1024], P('dp', 'seq')
- grad_wo: float32 [1024, 1024], P('seq', 'dp')
The draws below stay inside these ranges and needn't reach their ends.
Inputs may be any that keep to these rules, and one draw needn't show every extreme that they name: `key_blocks`: row b of a sequence's lists holds 16 distinct block numbers, the first of them b itself; entries past block_counts are valid numbers and are not used. `block_counts`: every sequence has a query block with exactly 16 used entries.
All inputs are finite; a program needn't handle non-finite values.
Results may differ from the reference program's by a relative error of at most 0.039.
Values may be sent and summed in bfloat16 or wider, within the bound.
No kernel may reach another device: no remote copies, remote signals or barrier semaphores. Data moves between devices by JAX's collectives and lax.ppermute only.
A program may use at most 128 MiB of HBM per device.

```python
import math
import jax
import jax.numpy as jnp
from jax import lax

D = 1024
HEADS = 16
REPLICAS = 16
NODES = 4096
BLOCKS = 32
LISTED = 16


def draw_queries(key, part):
    key = jax.random.fold_in(key, 3)
    field = jnp.clip(jax.random.normal(key, (REPLICAS, NODES, D), jnp.float32), -6.0, 6.0)
    return field.astype(jnp.bfloat16)


def draw_keys(key, part):
    key = jax.random.fold_in(key, 4)
    field = jnp.clip(jax.random.normal(key, (REPLICAS, NODES, D), jnp.float32), -6.0, 6.0)
    return field.astype(jnp.bfloat16)


def draw_key_blocks(key, part):
    key = jax.random.fold_in(key, 5)
    split_keys = jax.random.split(key, REPLICAS * BLOCKS)
    shuffled = jax.vmap(lambda single: jax.random.permutation(single, BLOCKS - 1))(split_keys) + 1
    offsets = jnp.concatenate([jnp.zeros((REPLICAS * BLOCKS, 1), jnp.int32), shuffled.astype(jnp.int32)], axis=1)[:, :LISTED]
    starts = jnp.tile(jnp.arange(BLOCKS, dtype=jnp.int32), REPLICAS)[:, None]
    return ((starts + offsets) % BLOCKS).reshape(REPLICAS, BLOCKS, LISTED).astype(jnp.int32)


def draw_block_counts(key, part):
    key = jax.random.fold_in(key, 7)
    first, second = jax.random.split(key)
    counts = jax.random.randint(first, (REPLICAS, BLOCKS), 1, LISTED + 1)
    heavy = jax.random.randint(second, (REPLICAS,), 0, BLOCKS)
    counts = jnp.where(jnp.arange(BLOCKS)[None, :] == heavy[:, None], LISTED, counts)
    return counts.astype(jnp.int32)


def with_spikes(values, key, source, target, shards_of, factor):
    def block_of(position):
        return (jnp.arange(values.shape[position]) // (values.shape[position] // shards_of)).reshape((-1,) + (1,) * (values.ndim - 1 - position))

    near = jax.random.permutation(key, shards_of)[block_of(target)]
    far = (block_of(target) + shards_of // 2) % shards_of
    return jnp.where((block_of(source) == near) | (block_of(source) == far), factor * values, values)


def block_scale(key, shape, cuts, least, top_value):
    def one(dim, shards_of):
        heights = jax.random.uniform(jax.random.fold_in(jax.random.fold_in(key, 6), dim), (shards_of,), jnp.float32, least / len(cuts), top_value / len(cuts))
        return jnp.repeat(jnp.exp(heights), shape[dim] // shards_of).reshape((-1,) + (1,) * (len(shape) - dim - 1))

    gain = one(*cuts[0])
    for cut in cuts[1:]:
        gain = gain * one(*cut)
    return gain


def scatter_about(key, extent, scale, reach, shards=(), held_as=jnp.bfloat16):
    level = block_scale(key, extent, shards, -0.22, 0.18) if shards else 1.0
    drawn = jax.random.normal(key, extent, jnp.float32) * scale * level
    return jnp.minimum(jnp.maximum(drawn, -reach), reach).astype(held_as)


def noise_with(rng, dims, deviation, bound, pieces, heavy, kind=jnp.bfloat16):
    entries = deviation * jax.random.normal(rng, dims, jnp.float32)
    if pieces:
        entries = entries * block_scale(rng, dims, pieces, -0.22, 0.18)
    return jnp.clip(with_spikes(entries, jax.random.fold_in(rng, 3), *heavy), -bound, bound).astype(kind)


def setup_inputs(seed: int = 0) -> dict:
    splits = jax.random.split(jax.random.key(seed), 8)
    queries = draw_queries(jax.random.fold_in(splits[7], 71), 0)
    keys = draw_keys(jax.random.fold_in(splits[7], 71), 0)
    values = scatter_about(splits[2], (REPLICAS, NODES, D), 3.0, 12.0, ((0, 16), (1, 16)))
    upstream = noise_with(splits[3], (REPLICAS, NODES, D), 1.0, 6.0, ((0, 16), (1, 16)), (0, 2, 16, 2.0))
    w_out = scatter_about(splits[4], (D, D), D ** -0.5, 0.1875)
    key_blocks = draw_key_blocks(jax.random.fold_in(splits[7], 71), 0)
    block_counts = draw_block_counts(jax.random.fold_in(splits[7], 71), 0)
    return dict(queries=queries, keys=keys, values=values, upstream=upstream, w_out=w_out, key_blocks=key_blocks, block_counts=block_counts)


blocks_per_step = 4

def product(form, left, right):
    return jnp.einsum(form, left.astype(jnp.float32), right.astype(jnp.float32), precision=lax.Precision.HIGHEST)

def block_attention(head_q, head_k, head_v, head_g, key_lists, key_counts):
    node_count, head_count, head_width = head_q.shape
    block_count, listed = key_lists.shape
    block_rows = node_count // block_count
    steps_count = block_count // blocks_per_step
    score_scale = 1.0 / math.sqrt(head_width)
    query_groups = head_q.reshape(steps_count, blocks_per_step, block_rows, head_count, head_width)
    grad_groups = head_g.reshape(steps_count, blocks_per_step, block_rows, head_count, head_width)
    key_table = head_k.reshape(block_count, block_rows, head_count, head_width)
    value_table = head_v.reshape(block_count, block_rows, head_count, head_width)
    list_groups = key_lists.reshape(steps_count, blocks_per_step, listed)
    count_groups = key_counts.reshape(steps_count, blocks_per_step)
    slot_index = jnp.arange(listed, dtype=jnp.int32)

    def one_step(accumulated, inputs):
        key_acc, value_acc = accumulated
        query_part, grad_part, list_part, count_part = inputs
        keys_near = key_table[list_part]
        values_near = value_table[list_part]
        scores = product('gqnd,gjknd->gnqjk', query_part, keys_near) * score_scale
        usable = (slot_index[None, :] < count_part[:, None])[:, None, None, :, None]
        scores = jnp.where(usable, scores, -jnp.inf)
        highest = lax.optimization_barrier(jnp.max(scores, axis=(3, 4), keepdims=True))
        raised = jnp.exp(scores - highest)
        probability = raised / lax.optimization_barrier(jnp.sum(raised, axis=(3, 4), keepdims=True))
        weights = probability.astype(jnp.bfloat16)
        attended = product('gnqjk,gjknd->gqnd', weights, values_near).astype(jnp.bfloat16)
        row_delta = lax.optimization_barrier(jnp.sum(grad_part.astype(jnp.float32) * attended.astype(jnp.float32), axis=3))
        grad_scores = product('gqnd,gjknd->gnqjk', grad_part, values_near)
        shifted = grad_scores - jnp.transpose(row_delta, (0, 2, 1))[:, :, :, None, None]
        grad_logits = (probability * shifted).astype(jnp.bfloat16)
        grad_query = (product('gnqjk,gjknd->gqnd', grad_logits, keys_near) * score_scale).astype(jnp.bfloat16)
        key_terms = product('gnqjk,gqnd->gjknd', grad_logits, query_part) * score_scale
        value_terms = product('gnqjk,gqnd->gjknd', weights, grad_part)
        flat_list = list_part.reshape(-1)
        key_acc = key_acc.at[flat_list].add(key_terms.reshape(-1, block_rows, head_count, head_width))
        value_acc = value_acc.at[flat_list].add(value_terms.reshape(-1, block_rows, head_count, head_width))
        return ((key_acc, value_acc), (attended, grad_query))
    empty = jnp.zeros((block_count, block_rows, head_count, head_width), jnp.float32)
    (key_acc, value_acc), (attended, grad_query) = lax.scan(one_step, (empty, empty), (query_groups, grad_groups, list_groups, count_groups))
    shape = (node_count, head_count, head_width)
    return (attended.reshape(shape), grad_query.reshape(shape), key_acc.astype(jnp.bfloat16).reshape(shape), value_acc.astype(jnp.bfloat16).reshape(shape))

def reference(queries, keys, values, upstream, w_out, key_blocks, block_counts):
    replica_count, node_count, width = queries.shape
    head_width = width // HEADS
    up_flat = upstream.reshape(-1, width)
    grad_att = jnp.dot(up_flat, w_out.T, preferred_element_type=jnp.float32).astype(jnp.bfloat16)

    def split_heads(array):
        return array.reshape(replica_count, node_count, HEADS, head_width)

    def per_replica(inputs):
        return block_attention(*inputs)
    attended, grad_query, grad_key, grad_value = lax.map(per_replica, (split_heads(queries), split_heads(keys), split_heads(values), split_heads(grad_att.reshape(replica_count, node_count, width)), key_blocks, block_counts))
    full_shape = (replica_count, node_count, width)
    att_flat = attended.reshape(-1, width)
    mixed = jnp.dot(att_flat, w_out, preferred_element_type=jnp.float32).astype(jnp.bfloat16).reshape(full_shape)
    grad_wo = jnp.dot(att_flat.T, up_flat, preferred_element_type=jnp.float32) * (1.0 / math.sqrt(replica_count * node_count))
    return (mixed, grad_query.reshape(full_shape), grad_key.reshape(full_shape), grad_value.reshape(full_shape), grad_wo)
```

```python
import math

import jax
import jax.numpy as jnp
from jax import lax
from jax.experimental import pallas as pl
from jax.experimental.pallas import tpu as pltpu
from jax.sharding import PartitionSpec as P

HEADS = 16
HEAD_WIDTH = 64
BLOCK_ROWS = 128
LANES = 2 * HEAD_WIDTH
SLOTS_PER_STEP = 4
MASKED = -1e30
SCORE_SCALE = 1.0 / math.sqrt(HEAD_WIDTH)
EXP2_SCALE = SCORE_SCALE * math.log2(math.e)

VMEM_SPEC = pl.BlockSpec(memory_space=pltpu.VMEM)
SMEM_SPEC = pl.BlockSpec(memory_space=pltpu.SMEM)


def dot(left, right, contract):
    return lax.dot_general(
        left, right, (contract, ((), ())), preferred_element_type=jnp.float32
    )


def head_columns(head):
    return slice(head * HEAD_WIDTH, (head + 1) * HEAD_WIDTH)


def pair_columns(left_ref, right, out_ref):
    for head in range(HEADS):
        columns = head_columns(head)
        out_ref[head] = jnp.concatenate([left_ref[:, columns], right[:, columns]], axis=1)


def pack_keys_values(key_ref, value_ref, out_ref):
    pair_columns(key_ref, value_ref, out_ref)


def pack_queries_grads(query_ref, up_ref, wo_ref, out_ref):
    grad = dot(up_ref[...], wo_ref[...], ((1,), (1,))).astype(jnp.bfloat16)
    pair_columns(query_ref, grad, out_ref)


def attention_kernel(
    list_ref, count_ref, kv_ref, qg_ref, ga_ref, gkv_ref, kv_turned, score_buf, gkv_acc
):
    blocks = kv_ref.shape[0]
    group_rows = SLOTS_PER_STEP * BLOCK_ROWS
    lane = lax.broadcasted_iota(jnp.int32, (BLOCK_ROWS, LANES), 1)
    low = lane < HEAD_WIDTH

    def prepare(block, _):
        kv_turned[block] = kv_ref[block].T
        gkv_acc[block] = jnp.zeros((BLOCK_ROWS, LANES), jnp.float32)
        return 0

    lax.fori_loop(0, blocks, prepare, 0)

    def one_query_block(block, _):
        count = count_ref[block]
        groups = (count + SLOTS_PER_STEP - 1) // SLOTS_PER_STEP
        qg = qg_ref[block]
        zero = jnp.zeros_like(qg)
        qg_split = jnp.concatenate([jnp.where(low, qg, zero), jnp.where(low, zero, qg)], axis=0)

        def score_step(group, highest):
            for unit in range(SLOTS_PER_STEP):
                slot = group * SLOTS_PER_STEP + unit
                both = dot(kv_ref[list_ref[block, slot]], qg_split, ((1,), (1,)))
                scores = jnp.where(slot < count, both[:, :BLOCK_ROWS], MASKED)
                rows = pl.ds(pl.multiple_of(slot * BLOCK_ROWS, BLOCK_ROWS), BLOCK_ROWS)
                score_buf[rows, :BLOCK_ROWS] = scores
                score_buf[rows, BLOCK_ROWS:] = both[:, BLOCK_ROWS:]
                highest = jnp.maximum(highest, jnp.max(scores.reshape(-1, 8, BLOCK_ROWS), axis=0))
            return highest

        highest = lax.fori_loop(
            0, groups, score_step, jnp.full((8, BLOCK_ROWS), MASKED, jnp.float32)
        )
        highest = jnp.max(highest, axis=0, keepdims=True)

        def raise_step(group, sums):
            total, weighted = sums
            rows = pl.ds(pl.multiple_of(group * group_rows, group_rows), group_rows)
            raised = jnp.exp2((score_buf[rows, :BLOCK_ROWS] - highest) * EXP2_SCALE)
            score_buf[rows, :BLOCK_ROWS] = raised
            total = total + jnp.sum(raised.reshape(-1, 8, BLOCK_ROWS), axis=0)
            terms = raised * score_buf[rows, BLOCK_ROWS:]
            weighted = weighted + jnp.sum(terms.reshape(-1, 8, BLOCK_ROWS), axis=0)
            return total, weighted

        empty = jnp.zeros((8, BLOCK_ROWS), jnp.float32)
        total, weighted = lax.fori_loop(0, groups, raise_step, (empty, empty))
        inverse = 1.0 / jnp.sum(total, axis=0, keepdims=True)
        row_delta = jnp.sum(weighted, axis=0, keepdims=True) * inverse

        def grad_step(group, sums):
            grad_q, attended = sums
            for half in range(SLOTS_PER_STEP // 2):
                slot = group * SLOTS_PER_STEP + 2 * half
                rows = pl.ds(pl.multiple_of(slot * BLOCK_ROWS, 2 * BLOCK_ROWS), 2 * BLOCK_ROWS)
                first, second = list_ref[block, slot], list_ref[block, slot + 1]
                probability = score_buf[rows, :BLOCK_ROWS] * inverse
                logits = probability * (score_buf[rows, BLOCK_ROWS:] - row_delta)
                joined = jnp.concatenate([logits, probability], axis=1).astype(jnp.bfloat16)
                key_terms = dot(joined, qg_split, ((1,), (0,)))
                gkv_acc[first] += key_terms[:BLOCK_ROWS]
                gkv_acc[second] += key_terms[BLOCK_ROWS:]
                turned = jnp.concatenate([kv_turned[first], kv_turned[second]], axis=1)
                query_terms = dot(turned, joined, ((1,), (0,)))
                grad_q = grad_q + query_terms[:HEAD_WIDTH, :BLOCK_ROWS]
                attended = attended + query_terms[HEAD_WIDTH:, BLOCK_ROWS:]
            return grad_q, attended

        empty = jnp.zeros((HEAD_WIDTH, BLOCK_ROWS), jnp.float32)
        grad_q, attended = lax.fori_loop(0, groups, grad_step, (empty, empty))
        turned = jnp.concatenate([grad_q * SCORE_SCALE, attended], axis=0)
        ga_ref[block] = turned.T.astype(jnp.bfloat16)
        return 0

    lax.fori_loop(0, blocks, one_query_block, 0)

    scale = jnp.where(low, SCORE_SCALE, 1.0)

    def finish(block, _):
        gkv_ref[block] = (gkv_acc[block] * scale).astype(jnp.bfloat16)
        return 0

    lax.fori_loop(0, blocks, finish, 0)


def finish_kernel(
    core_ref, ga_ref, gkv_ref, up_ref, wo_ref, mixed_ref, gq_ref, gk_ref, gv_ref, keep_ref, send_ref
):
    attended = []
    for head in range(HEADS):
        columns = head_columns(head)
        gq_ref[:, columns] = ga_ref[head, :, :HEAD_WIDTH]
        gk_ref[:, columns] = gkv_ref[head, :, :HEAD_WIDTH]
        gv_ref[:, columns] = gkv_ref[head, :, HEAD_WIDTH:]
        attended.append(ga_ref[head, :, HEAD_WIDTH:])
    attended = jnp.concatenate(attended, axis=1)
    mixed_ref[...] = dot(attended, wo_ref[...], ((1,), (0,))).astype(jnp.bfloat16)
    pieces = up_ref.shape[1] // HEAD_WIDTH
    even = jnp.concatenate([up_ref[:, head_columns(i)] for i in range(0, pieces, 2)], axis=1)
    odd = jnp.concatenate([up_ref[:, head_columns(i)] for i in range(1, pieces, 2)], axis=1)
    first = core_ref[0] == 0
    own = jnp.where(first, even, odd)
    other = jnp.where(first, odd, even)
    keep_ref[...] = dot(attended, own, ((0,), (0,)))
    send_ref[...] = dot(attended, other, ((0,), (0,))).astype(jnp.bfloat16)


def local(queries, keys, values, upstream, w_out, key_blocks, block_counts):
    local_rows, width = queries.shape[1:]
    seq_size, dp_size = lax.axis_size("seq"), lax.axis_size("dp")
    blocks = block_counts.shape[1]
    node_count = local_rows * seq_size
    up_rows = upstream[0]
    packed = jax.ShapeDtypeStruct((HEADS, local_rows, LANES), jnp.bfloat16)
    by_block = (blocks, BLOCK_ROWS, LANES)
    params = pltpu.CompilerParams(vmem_limit_bytes=48 * 2**20)

    kv_send = pl.pallas_call(
        pack_keys_values,
        out_shape=packed,
        in_specs=[VMEM_SPEC] * 2,
        out_specs=VMEM_SPEC,
        compiler_params=params,
    )(keys[0], values[0])
    kv = lax.all_to_all(kv_send, "seq", split_axis=0, concat_axis=0, tiled=True)
    qg_send = pl.pallas_call(
        pack_queries_grads,
        out_shape=packed,
        in_specs=[VMEM_SPEC] * 3,
        out_specs=VMEM_SPEC,
        compiler_params=params,
    )(queries[0], up_rows, w_out)
    qg = lax.all_to_all(qg_send, "seq", split_axis=0, concat_axis=0, tiled=True)

    ga, gkv = pl.pallas_call(
        attention_kernel,
        out_shape=[jax.ShapeDtypeStruct(by_block, jnp.bfloat16)] * 2,
        in_specs=[SMEM_SPEC, SMEM_SPEC, VMEM_SPEC, VMEM_SPEC],
        out_specs=[VMEM_SPEC] * 2,
        scratch_shapes=[
            pltpu.VMEM((blocks, LANES, BLOCK_ROWS), jnp.bfloat16),
            pltpu.VMEM((key_blocks.shape[2] * BLOCK_ROWS, 2 * BLOCK_ROWS), jnp.float32),
            pltpu.VMEM(by_block, jnp.float32),
        ],
        compiler_params=params,
    )(key_blocks[0], block_counts[0], kv.reshape(by_block), qg.reshape(by_block))

    by_head = (HEADS, local_rows, LANES)
    ga = lax.all_to_all(ga.reshape(by_head), "seq", split_axis=0, concat_axis=0, tiled=True)
    gkv = lax.all_to_all(gkv.reshape(by_head), "seq", split_axis=0, concat_axis=0, tiled=True)

    core = lax.axis_index("dp") % 2
    half = width // 2
    rows = jax.ShapeDtypeStruct((local_rows, width), jnp.bfloat16)
    mixed, gq, gk, gv, keep, send = pl.pallas_call(
        finish_kernel,
        out_shape=[
            rows,
            rows,
            rows,
            rows,
            jax.ShapeDtypeStruct((width, half), jnp.float32),
            jax.ShapeDtypeStruct((width, half), jnp.bfloat16),
        ],
        in_specs=[SMEM_SPEC] + [VMEM_SPEC] * 4,
        out_specs=[VMEM_SPEC] * 6,
        compiler_params=params,
    )(core.reshape(1).astype(jnp.int32), ga, gkv, up_rows, w_out)

    other_core = [(i, i + 1 - 2 * (i % 2)) for i in range(dp_size)]
    chips = dp_size // 2
    same_core = [[2 * z + c for z in range(chips)] for c in range(2)]
    chip_sum = (keep + lax.ppermute(send, "dp", other_core).astype(jnp.float32)).astype(jnp.bfloat16)
    parts = lax.all_to_all(
        chip_sum.reshape(seq_size, width // seq_size, half), "seq", split_axis=0, concat_axis=0, tiled=True
    )
    seq_sum = jnp.sum(parts.astype(jnp.float32), axis=0).astype(jnp.bfloat16)
    seq_sum = jnp.swapaxes(seq_sum.reshape(width // seq_size, chips, half // chips), 0, 1)
    terms = lax.all_to_all(
        seq_sum, "dp", split_axis=0, concat_axis=0, axis_index_groups=same_core, tiled=True
    )
    factor = 1.0 / math.sqrt(dp_size * node_count)
    grad_wo = jnp.sum(terms.astype(jnp.float32), axis=0) * factor
    full_shape = (1, local_rows, width)
    return (
        mixed.reshape(full_shape),
        gq.reshape(full_shape),
        gk.reshape(full_shape),
        gv.reshape(full_shape),
        grad_wo,
    )


def solution(mesh):
    placed = (
        P("dp", "seq", None),
        P("dp", "seq", None),
        P("dp", "seq", None),
        P("dp", "seq", None),
        P(),
        P("dp", None, None),
        P("dp", None),
    )
    return jax.shard_map(
        local,
        mesh=mesh,
        in_specs=placed,
        out_specs=(
            P("dp", "seq", None),
            P("dp", "seq", None),
            P("dp", "seq", None),
            P("dp", "seq", None),
            P("seq", "dp"),
        ),
        check_vma=False,
    )
```

```python
import functools
import math

import jax
import jax.numpy as jnp
from jax import lax
from jax.experimental import pallas as pl
from jax.experimental.pallas import tpu as pltpu
from jax.sharding import PartitionSpec as P

HEADS = 16
HEAD_WIDTH = 64
BLOCK_ROWS = 128
LANES = 2 * HEAD_WIDTH
FORWARD_TILE = 4
BACKWARD_TILE = 2
SLOT_STEP = 2
FIRST_TILES = 4
MASKED = -1e30
SCORE_SCALE = 1.0 / math.sqrt(HEAD_WIDTH)
EXP2_SCALE = SCORE_SCALE * math.log2(math.e)

VMEM_SPEC = pl.BlockSpec(memory_space=pltpu.VMEM)
SMEM_SPEC = pl.BlockSpec(memory_space=pltpu.SMEM)


def dot(left, right, contract):
    return lax.dot_general(
        left, right, (contract, ((), ())), preferred_element_type=jnp.float32
    )


def call(kernel, name, outs, in_specs, scratch=(), flops=0, **kwargs):
    return pl.pallas_call(
        kernel,
        out_shape=outs,
        in_specs=in_specs,
        out_specs=[VMEM_SPEC] * len(outs),
        scratch_shapes=list(scratch),
        compiler_params=pltpu.CompilerParams(vmem_limit_bytes=24 * 2**20),
        cost_estimate=pl.CostEstimate(flops=flops, bytes_accessed=4 * 2**20, transcendentals=0),
        name=name,
        **kwargs,
    )


def pack_kernel(query_ref, key_ref, value_ref, up_ref, wo_ref, out_ref):
    grads = dot(up_ref[...], wo_ref[...], ((1,), (1,))).astype(jnp.bfloat16)
    heads_here = out_ref.shape[0]
    for head in range(heads_here):
        columns = slice(head * HEAD_WIDTH, (head + 1) * HEAD_WIDTH)
        kv = jnp.concatenate([key_ref[:, columns], value_ref[:, columns]], axis=1)
        qg = jnp.concatenate([query_ref[:, columns], grads[:, columns]], axis=1)
        for block in range(out_ref.shape[1]):
            rows = slice(block * BLOCK_ROWS, (block + 1) * BLOCK_ROWS)
            out_ref[head, block, :BLOCK_ROWS] = kv[rows]
            out_ref[head, block, BLOCK_ROWS:] = qg[rows]


def pack(queries, keys, values, up_rows, w_out):
    rows, width = queries.shape
    blocks = rows // BLOCK_ROWS
    steps = 4
    columns = width // steps
    part = pl.BlockSpec((rows, columns), lambda i: (0, i))
    return pl.pallas_call(
        pack_kernel,
        grid=(steps,),
        out_shape=jax.ShapeDtypeStruct((HEADS, blocks, 2 * BLOCK_ROWS, LANES), jnp.bfloat16),
        in_specs=[
            part,
            part,
            part,
            pl.BlockSpec((rows, width), lambda i: (0, 0)),
            pl.BlockSpec((columns, width), lambda i: (i, 0)),
        ],
        out_specs=pl.BlockSpec(
            (HEADS // steps, blocks, 2 * BLOCK_ROWS, LANES), lambda i: (i, 0, 0, 0)
        ),
        compiler_params=pltpu.CompilerParams(vmem_limit_bytes=60 * 2**20),
        name="pack",
    )(queries, keys, values, up_rows, w_out)


def for_tiles(tiles, tile_blocks, listed, order_ref, count_ref, process):
    def one_tile(tile, _):
        members = [order_ref[tile * tile_blocks + i] for i in range(tile_blocks)]
        steps = (count_ref[members[0]] + SLOT_STEP - 1) // SLOT_STEP
        sizes = range(SLOT_STEP, listed + 1, SLOT_STEP)
        lax.switch(steps - 1, [functools.partial(process, members, size) for size in sizes])
        return 0

    lax.fori_loop(*tiles, one_tile, 0)


def by_fours(blocks, body):
    def four(index, _):
        for unit in range(4):
            body(4 * index + unit)
        return 0

    lax.fori_loop(0, blocks // 4, four, 0)


def forward_kernel(list_ref, count_ref, order_ref, in_ref, att_ref, stat_ref, turned, *score_bufs):
    blocks, listed = list_ref.shape
    low = lax.broadcasted_iota(jnp.int32, (LANES, BLOCK_ROWS), 0) < HEAD_WIDTH

    def turn(block):
        turned[block] = in_ref[block, :BLOCK_ROWS].T[HEAD_WIDTH:]

    by_fours(blocks, turn)

    def process(members, slots):
        qg_turned = [in_ref[block, BLOCK_ROWS:].T for block in members]
        queries = [jnp.where(low, array, jnp.zeros_like(array)) for array in qg_turned]
        near = [[list_ref[block, slot] for slot in range(slots)] for block in members]
        highest = []
        for i, block in enumerate(members):
            rows = jnp.concatenate([in_ref[key, :BLOCK_ROWS] for key in near[i]], axis=0)
            scores = dot(rows, queries[i], ((1,), (0,)))
            top = jnp.full((8, BLOCK_ROWS), MASKED, jnp.float32)
            for slot in range(slots):
                here = slice(slot * BLOCK_ROWS, (slot + 1) * BLOCK_ROWS)
                part = jnp.where(slot < count_ref[block], scores[here], MASKED)
                score_bufs[i][here] = part
                top = jnp.maximum(top, jnp.max(part.reshape(-1, 8, BLOCK_ROWS), axis=0))
            highest.append(jnp.max(top, axis=0, keepdims=True))
        for i, block in enumerate(members):
            part = score_bufs[i][: slots * BLOCK_ROWS]
            raised = jnp.exp2((part - highest[i]) * EXP2_SCALE)
            total = jnp.sum(raised, axis=0, keepdims=True)
            flat = jnp.concatenate([turned[key] for key in near[i]], axis=1)
            sums = dot(flat, raised.astype(jnp.bfloat16), ((1,), (0,)))
            attended = (sums * (1.0 / total)).astype(jnp.bfloat16)
            att_ref[block] = attended
            grads = qg_turned[i][HEAD_WIDTH:].astype(jnp.float32)
            delta = jnp.sum(attended.astype(jnp.float32) * grads, axis=0, keepdims=True)
            stat_ref[block, 0:1] = highest[i] + jnp.log2(total) * (1.0 / EXP2_SCALE)
            stat_ref[block, 1:2] = delta

    for_tiles(
        (0, blocks // FORWARD_TILE), FORWARD_TILE, listed, order_ref, count_ref, process
    )


def backward_kernel(tiles, first, list_ref, count_ref, order_ref, in_ref, stat_ref, *refs):
    if first:
        out_ref, acc_ref, turned = refs
    else:
        gq_before, acc_before, out_ref, turned, acc_ref = refs
    blocks, listed = list_ref.shape
    low_lanes = lax.broadcasted_iota(jnp.int32, (BLOCK_ROWS, LANES), 1) < HEAD_WIDTH
    low_rows = lax.broadcasted_iota(jnp.int32, (LANES, BLOCK_ROWS), 0) < HEAD_WIDTH

    def prepare(block):
        turned[block] = in_ref[block, :BLOCK_ROWS].T[:HEAD_WIDTH]
        if first:
            acc_ref[block] = jnp.zeros((BLOCK_ROWS, LANES), jnp.float32)
        else:
            acc_ref[block] = acc_before[block]
            out_ref[block, :HEAD_WIDTH] = gq_before[block]

    by_fours(blocks, prepare)

    def process(members, slots):
        for block in members:
            qg = in_ref[block, BLOCK_ROWS:]
            flat = qg.T
            zero = jnp.zeros_like(qg)
            across = jnp.concatenate(
                [jnp.where(low_rows, flat, zero), jnp.where(low_rows, zero, flat)], axis=1
            )
            down = jnp.concatenate(
                [jnp.where(low_lanes, qg, zero), jnp.where(low_lanes, zero, qg)], axis=0
            )
            top, delta = stat_ref[block, 0:1], stat_ref[block, 1:2]
            near = [list_ref[block, slot] for slot in range(slots)]
            rows = jnp.concatenate([in_ref[key, :BLOCK_ROWS] for key in near], axis=0)
            both = dot(rows, across, ((1,), (0,)))
            joined = []
            for slot in range(slots):
                part = both[slot * BLOCK_ROWS : (slot + 1) * BLOCK_ROWS]
                probability = jnp.exp2((part[:, :BLOCK_ROWS] - top) * EXP2_SCALE)
                probability = jnp.where(slot < count_ref[block], probability, 0.0)
                logits = probability * (part[:, BLOCK_ROWS:] - delta)
                joined.append(
                    jnp.concatenate(
                        [logits.astype(jnp.bfloat16), probability.astype(jnp.bfloat16)], axis=1
                    )
                )
            joined = jnp.concatenate(joined, axis=0)
            key_terms = dot(joined, down, ((1,), (0,)))
            for slot, key in enumerate(near):
                acc_ref[key] += key_terms[slot * BLOCK_ROWS : (slot + 1) * BLOCK_ROWS]
            flat = jnp.concatenate([turned[key] for key in near], axis=1)
            grads = dot(flat, joined[:, :BLOCK_ROWS], ((1,), (0,)))
            out_ref[block, :HEAD_WIDTH] = (grads * SCORE_SCALE).astype(jnp.bfloat16)

    for_tiles(tiles, BACKWARD_TILE, listed, order_ref, count_ref, process)
    if first:
        return
    scale = jnp.where(low_lanes, SCORE_SCALE, 1.0)

    def finish(block):
        out_ref[block, HEAD_WIDTH:] = (acc_ref[block] * scale).astype(jnp.bfloat16)

    by_fours(blocks, finish)


def weight_grad_kernel(core_ref, att_ref, up_ref, keep_ref, send_ref):
    attended = attended_columns(att_ref)
    pieces = up_ref.shape[1] // HEAD_WIDTH

    def every_other(start):
        return jnp.concatenate(
            [up_ref[:, i * HEAD_WIDTH : (i + 1) * HEAD_WIDTH] for i in range(start, pieces, 2)],
            axis=1,
        )

    even, odd = every_other(0), every_other(1)
    first = core_ref[0] == 0
    send_ref[...] = dot(attended, jnp.where(first, odd, even), ((1,), (0,))).astype(jnp.bfloat16)
    keep_ref[...] = dot(attended, jnp.where(first, even, odd), ((1,), (0,)))


def attended_columns(att_ref):
    heads, blocks = att_ref.shape[:2]
    return jnp.concatenate(
        [
            jnp.concatenate([att_ref[head, block] for head in range(heads)], axis=0)
            for block in range(blocks)
        ],
        axis=1,
    )


def mixed_kernel(att_ref, wo_ref, mixed_ref):
    attended = attended_columns(att_ref).T
    mixed_ref[...] = dot(attended, wo_ref[...], ((1,), (0,))).astype(jnp.bfloat16)


def unpack_kernel(in_ref, gq_ref, gk_ref, gv_ref):
    blocks = in_ref.shape[1]
    low = lax.broadcasted_iota(jnp.int32, (BLOCK_ROWS, LANES), 1) < HEAD_WIDTH
    for block in range(blocks):
        rows = slice(block * BLOCK_ROWS, (block + 1) * BLOCK_ROWS)
        for head in range(0, HEADS, 2):
            columns = slice(head * HEAD_WIDTH, (head + 2) * HEAD_WIDTH)
            flat = jnp.concatenate([in_ref[head + i, block, :HEAD_WIDTH] for i in range(2)], axis=0)
            gq_ref[rows, columns] = flat.T
            one, two = (in_ref[head + i, block, HEAD_WIDTH:] for i in range(2))
            gk_ref[rows, columns] = jnp.concatenate(
                [one[:, :HEAD_WIDTH], two[:, :HEAD_WIDTH]], axis=1
            )
            gv_ref[rows, columns] = jnp.concatenate(
                [one[:, HEAD_WIDTH:], two[:, HEAD_WIDTH:]], axis=1
            )


def by_falling_count(counts):
    index = jnp.arange(counts.shape[0], dtype=jnp.int32)
    place = -counts * counts.shape[0] + index
    rank = jnp.sum((place[None, :] < place[:, None]).astype(jnp.int32), axis=1)
    return jnp.sum(jnp.where(rank[None, :] == index[:, None], index[None, :], 0), axis=1)


def exchange(array):
    return lax.all_to_all(array, "seq", split_axis=0, concat_axis=0, tiled=True)


def local(queries, keys, values, upstream, w_out, key_blocks, block_counts):
    local_rows, width = queries.shape[1:]
    seq_size, dp_size = lax.axis_size("seq"), lax.axis_size("dp")
    lists, counts = key_blocks[0], block_counts[0]
    blocks, listed = lists.shape
    near_blocks = local_rows // BLOCK_ROWS
    up_rows = upstream[0]
    bf16, f32 = jnp.bfloat16, jnp.float32
    shape = jax.ShapeDtypeStruct
    smem, vmem = SMEM_SPEC, VMEM_SPEC

    packed = exchange(pack(queries[0], keys[0], values[0], up_rows, w_out))
    packed = packed.reshape(blocks, 2 * BLOCK_ROWS, LANES)
    lists, counts, order = lax.optimization_barrier((lists, counts, by_falling_count(counts)))
    listing = (lists, counts, order)
    turned = pltpu.VMEM((blocks, HEAD_WIDTH, BLOCK_ROWS), bf16)
    acc = (blocks, BLOCK_ROWS, LANES)
    half_turned = shape((blocks, HEAD_WIDTH, BLOCK_ROWS), bf16)

    attended, stats = call(
        forward_kernel,
        "forward",
        [half_turned, shape((blocks, 8, BLOCK_ROWS), f32)],
        [smem] * 3 + [vmem],
        [turned] + [pltpu.VMEM((listed * BLOCK_ROWS, BLOCK_ROWS), f32)] * FORWARD_TILE,
        flops=10 * 10**9,
    )(*listing, packed)

    attended = exchange(attended.reshape(seq_size, near_blocks, HEAD_WIDTH, BLOCK_ROWS))
    first = call(
        functools.partial(backward_kernel, (0, FIRST_TILES), True),
        "backward_first",
        [half_turned, shape(acc, f32)],
        [smem] * 3 + [vmem] * 2,
        [turned],
        flops=10 * 10**9,
    )(*listing, packed, stats)

    attended, first = lax.optimization_barrier((attended, first))
    half = width // 2
    core = (lax.axis_index("dp") % 2).reshape(1).astype(jnp.int32)
    keep, send = call(
        weight_grad_kernel,
        "weight_grad",
        [shape((width, half), f32), shape((width, half), bf16)],
        [smem] + [vmem] * 2,
        flops=10**9,
    )(core, attended, up_rows)
    other_core = [(i, i + 1 - 2 * (i % 2)) for i in range(dp_size)]
    received = lax.ppermute(send, "dp", other_core)
    chip_sum = (keep + received.astype(f32)).astype(bf16)

    chip_sum, first, attended = lax.optimization_barrier((chip_sum, first, attended))
    parts = exchange(chip_sum.reshape(seq_size, width // seq_size, half))
    (outgoing,) = call(
        functools.partial(backward_kernel, (FIRST_TILES, blocks // BACKWARD_TILE), False),
        "backward_second",
        [shape((blocks, HEAD_WIDTH + BLOCK_ROWS, LANES), bf16)],
        [smem] * 3 + [vmem] * 4,
        [turned, pltpu.VMEM(acc, f32)],
        flops=15 * 10**9,
    )(*listing, packed, stats, *first)

    parts, outgoing = lax.optimization_barrier((parts, outgoing))
    seq_sum = jnp.sum(parts.astype(f32), axis=0).astype(bf16)
    incoming = exchange(
        outgoing.reshape(seq_size, near_blocks, HEAD_WIDTH + BLOCK_ROWS, LANES)
    )
    chips = dp_size // 2
    same_core = [[2 * z + c for z in range(chips)] for c in range(2)]
    seq_sum = jnp.swapaxes(seq_sum.reshape(width // seq_size, chips, half // chips), 0, 1)
    seq_sum, incoming = lax.optimization_barrier((seq_sum, incoming))
    terms = lax.all_to_all(
        seq_sum, "dp", split_axis=0, concat_axis=0, axis_index_groups=same_core, tiled=True
    )
    factor = 1.0 / math.sqrt(dp_size * local_rows * seq_size)
    grad_wo = jnp.sum(terms.astype(f32), axis=0) * factor

    rows = shape((local_rows, width), bf16)
    (mixed,) = call(mixed_kernel, "mixed", [rows], [vmem] * 2, flops=10**9)(attended, w_out)
    gq, gk, gv = call(unpack_kernel, "unpack", [rows] * 3, [vmem])(incoming)
    full_shape = (1, local_rows, width)
    return (
        mixed.reshape(full_shape),
        gq.reshape(full_shape),
        gk.reshape(full_shape),
        gv.reshape(full_shape),
        grad_wo,
    )


def solution(mesh):
    nodes = P("dp", "seq", None)
    return jax.shard_map(
        local,
        mesh=mesh,
        in_specs=(nodes, nodes, nodes, nodes, P(), P("dp", None, None), P("dp", None)),
        out_specs=(nodes, nodes, nodes, nodes, P("seq", "dp")),
        check_vma=False,
    )
```

```python
import functools
import math

import jax
import jax.numpy as jnp
from jax import lax
from jax.experimental import pallas as pl
from jax.experimental.pallas import tpu as pltpu
from jax.sharding import PartitionSpec as P

HEADS = 16
HEAD_WIDTH = 64
BLOCK_ROWS = 128
LANES = 2 * HEAD_WIDTH
FORWARD_TILE = 4
BACKWARD_TILE = 2
SLOT_STEP = 2
FIRST_TILES = 4
MASKED = -1e30
SCORE_SCALE = 1.0 / math.sqrt(HEAD_WIDTH)
EXP2_SCALE = SCORE_SCALE * math.log2(math.e)

HBM_SPEC = pl.BlockSpec(memory_space=pltpu.HBM)
VMEM_SPEC = pl.BlockSpec(memory_space=pltpu.VMEM)
SMEM_SPEC = pl.BlockSpec(memory_space=pltpu.SMEM)


def dot(left, right, contract):
    return lax.dot_general(
        left, right, (contract, ((), ())), preferred_element_type=jnp.float32
    )


def call(kernel, name, outs, in_specs, scratch=(), flops=0, out_specs=None, vmem=24):
    return pl.pallas_call(
        kernel,
        out_shape=outs,
        in_specs=in_specs,
        out_specs=out_specs or [VMEM_SPEC] * len(outs),
        scratch_shapes=list(scratch),
        compiler_params=pltpu.CompilerParams(vmem_limit_bytes=vmem * 2**20),
        cost_estimate=pl.CostEstimate(flops=flops, bytes_accessed=4 * 2**20, transcendentals=0),
        name=name,
    )


def pack_kernel(query_ref, key_ref, value_ref, up_ref, wo_ref, out_ref):
    grads = dot(up_ref[...], wo_ref[...], ((1,), (1,))).astype(jnp.bfloat16)
    heads_here = out_ref.shape[0]
    for head in range(heads_here):
        columns = slice(head * HEAD_WIDTH, (head + 1) * HEAD_WIDTH)
        kv = jnp.concatenate([key_ref[:, columns], value_ref[:, columns]], axis=1)
        qg = jnp.concatenate([query_ref[:, columns], grads[:, columns]], axis=1)
        for block in range(out_ref.shape[1]):
            rows = slice(block * BLOCK_ROWS, (block + 1) * BLOCK_ROWS)
            out_ref[head, block, :BLOCK_ROWS] = kv[rows]
            out_ref[head, block, BLOCK_ROWS:] = qg[rows]


def pack(queries, keys, values, up_rows, w_out):
    rows, width = queries.shape
    blocks = rows // BLOCK_ROWS
    steps = 2
    columns = width // steps
    part = pl.BlockSpec((rows, columns), lambda i: (0, i))
    return pl.pallas_call(
        pack_kernel,
        grid=(steps,),
        out_shape=jax.ShapeDtypeStruct((HEADS, blocks, 2 * BLOCK_ROWS, LANES), jnp.bfloat16),
        in_specs=[
            part,
            part,
            part,
            pl.BlockSpec((rows, width), lambda i: (0, 0)),
            pl.BlockSpec((columns, width), lambda i: (i, 0)),
        ],
        out_specs=pl.BlockSpec(
            (HEADS // steps, blocks, 2 * BLOCK_ROWS, LANES), lambda i: (i, 0, 0, 0)
        ),
        compiler_params=pltpu.CompilerParams(vmem_limit_bytes=60 * 2**20),
        name="pack",
    )(queries, keys, values, up_rows, w_out)


def for_tiles(tiles, tile_blocks, listed, order_ref, count_ref, process):
    def one_tile(tile, _):
        members = [order_ref[tile * tile_blocks + i] for i in range(tile_blocks)]
        steps = (count_ref[members[0]] + SLOT_STEP - 1) // SLOT_STEP
        sizes = range(SLOT_STEP, listed + 1, SLOT_STEP)
        lax.switch(steps - 1, [functools.partial(process, members, size) for size in sizes])
        return 0

    lax.fori_loop(*tiles, one_tile, 0)


def by_fours(blocks, body):
    def four(index, _):
        for unit in range(4):
            body(4 * index + unit)
        return 0

    lax.fori_loop(0, blocks // 4, four, 0)


def forward_kernel(list_ref, count_ref, order_ref, in_ref, att_ref, stat_ref, turned, *score_bufs):
    blocks, listed = list_ref.shape
    low = lax.broadcasted_iota(jnp.int32, (LANES, BLOCK_ROWS), 0) < HEAD_WIDTH

    def turn(block):
        turned[block] = in_ref[block, :BLOCK_ROWS].T[HEAD_WIDTH:]

    by_fours(blocks, turn)

    def process(members, slots):
        qg_turned = [in_ref[block, BLOCK_ROWS:].T for block in members]
        queries = [jnp.where(low, array, jnp.zeros_like(array)) for array in qg_turned]
        near = [[list_ref[block, slot] for slot in range(slots)] for block in members]
        highest = []
        for i, block in enumerate(members):
            rows = jnp.concatenate([in_ref[key, :BLOCK_ROWS] for key in near[i]], axis=0)
            scores = dot(rows, queries[i], ((1,), (0,)))
            top = jnp.full((8, BLOCK_ROWS), MASKED, jnp.float32)
            for slot in range(slots):
                here = slice(slot * BLOCK_ROWS, (slot + 1) * BLOCK_ROWS)
                part = jnp.where(slot < count_ref[block], scores[here], MASKED)
                score_bufs[i][here] = part
                top = jnp.maximum(top, jnp.max(part.reshape(-1, 8, BLOCK_ROWS), axis=0))
            highest.append(jnp.max(top, axis=0, keepdims=True))
        for i, block in enumerate(members):
            part = score_bufs[i][: slots * BLOCK_ROWS]
            raised = jnp.exp2((part - highest[i]) * EXP2_SCALE)
            total = jnp.sum(raised, axis=0, keepdims=True)
            flat = jnp.concatenate([turned[key] for key in near[i]], axis=1)
            sums = dot(flat, raised.astype(jnp.bfloat16), ((1,), (0,)))
            attended = (sums * (1.0 / total)).astype(jnp.bfloat16)
            att_ref[block] = attended
            grads = qg_turned[i][HEAD_WIDTH:].astype(jnp.float32)
            delta = jnp.sum(attended.astype(jnp.float32) * grads, axis=0, keepdims=True)
            stat_ref[block, 0:1] = highest[i] + jnp.log2(total) * (1.0 / EXP2_SCALE)
            stat_ref[block, 1:2] = delta

    for_tiles(
        (0, blocks // FORWARD_TILE), FORWARD_TILE, listed, order_ref, count_ref, process
    )


def backward_kernel(tiles, first, list_ref, count_ref, order_ref, in_ref, stat_ref, *refs):
    if first:
        out_ref, acc_out, token_ref, turned, acc_ref, sems = refs
    else:
        gq_before, acc_in, out_hbm, token_ref, turned, acc_ref, acc_before, out_ref, sems = refs
        fetch = pltpu.make_async_copy(acc_in, acc_before, sems.at[0])
        fetch.start()
    token_ref[...] = jnp.zeros_like(token_ref)
    blocks, listed = list_ref.shape
    low_lanes = lax.broadcasted_iota(jnp.int32, (BLOCK_ROWS, LANES), 1) < HEAD_WIDTH
    low_rows = lax.broadcasted_iota(jnp.int32, (LANES, BLOCK_ROWS), 0) < HEAD_WIDTH

    def prepare(block):
        turned[block] = in_ref[block, :BLOCK_ROWS].T[:HEAD_WIDTH]
        acc_ref[block] = jnp.zeros((BLOCK_ROWS, LANES), jnp.float32)

    by_fours(blocks, prepare)

    def process(members, slots):
        for block in members:
            qg = in_ref[block, BLOCK_ROWS:]
            flat = qg.T
            zero = jnp.zeros_like(qg)
            across = jnp.concatenate(
                [jnp.where(low_rows, flat, zero), jnp.where(low_rows, zero, flat)], axis=1
            )
            down = jnp.concatenate(
                [jnp.where(low_lanes, qg, zero), jnp.where(low_lanes, zero, qg)], axis=0
            )
            top, delta = stat_ref[block, 0:1], stat_ref[block, 1:2]
            near = [list_ref[block, slot] for slot in range(slots)]
            rows = jnp.concatenate([in_ref[key, :BLOCK_ROWS] for key in near], axis=0)
            both = dot(rows, across, ((1,), (0,)))
            joined = []
            for slot in range(slots):
                part = both[slot * BLOCK_ROWS : (slot + 1) * BLOCK_ROWS]
                probability = jnp.exp2((part[:, :BLOCK_ROWS] - top) * EXP2_SCALE)
                probability = jnp.where(slot < count_ref[block], probability, 0.0)
                logits = probability * (part[:, BLOCK_ROWS:] - delta)
                joined.append(
                    jnp.concatenate(
                        [logits.astype(jnp.bfloat16), probability.astype(jnp.bfloat16)], axis=1
                    )
                )
            joined = jnp.concatenate(joined, axis=0)
            key_terms = dot(joined, down, ((1,), (0,)))
            for slot, key in enumerate(near):
                acc_ref[key] += key_terms[slot * BLOCK_ROWS : (slot + 1) * BLOCK_ROWS]
            flat = jnp.concatenate([turned[key] for key in near], axis=1)
            grads = dot(flat, joined[:, :BLOCK_ROWS], ((1,), (0,)))
            out_ref[block, :HEAD_WIDTH] = (grads * SCORE_SCALE).astype(jnp.bfloat16)

    for_tiles(tiles, BACKWARD_TILE, listed, order_ref, count_ref, process)
    if first:
        store = pltpu.make_async_copy(acc_ref, acc_out, sems.at[0])
        store.start()
        store.wait()
        return
    for i in range(tiles[0] * BACKWARD_TILE):
        block = order_ref[i]
        out_ref[block, :HEAD_WIDTH] = gq_before[block]
    fetch.wait()
    scale = jnp.where(low_lanes, SCORE_SCALE, 1.0)

    def stores(chunk):
        here = pl.ds(4 * chunk, 4)
        return pltpu.make_async_copy(out_ref.at[here], out_hbm.at[here], sems.at[1 + chunk])

    for chunk in range(blocks // 4):
        for block in range(4 * chunk, 4 * chunk + 4):
            total = acc_ref[block] + acc_before[block]
            out_ref[block, HEAD_WIDTH:] = (total * scale).astype(jnp.bfloat16)
        stores(chunk).start()
    for chunk in range(blocks // 4):
        stores(chunk).wait()


def split_columns_kernel(core_ref, up_ref, keep_ref, send_ref):
    pieces = up_ref.shape[1] // HEAD_WIDTH

    def every_other(start):
        return jnp.concatenate(
            [up_ref[:, i * HEAD_WIDTH : (i + 1) * HEAD_WIDTH] for i in range(start, pieces, 2)],
            axis=1,
        )

    even, odd = every_other(0), every_other(1)
    first = core_ref[0] == 0
    keep_ref[...] = jnp.where(first, even, odd)
    send_ref[...] = jnp.where(first, odd, even)


def weight_grad_kernel(own_att_ref, other_att_ref, own_up_ref, other_up_ref, token_ref, out_ref):
    attended = jnp.concatenate(
        [attended_columns(own_att_ref), attended_columns(other_att_ref)], axis=1
    )
    up_rows = jnp.concatenate([own_up_ref[...], other_up_ref[...]], axis=0)
    out_ref[...] = dot(attended, up_rows, ((1,), (0,))).astype(jnp.bfloat16)


def attended_columns(att_ref):
    heads, blocks = att_ref.shape[:2]
    return jnp.concatenate(
        [
            jnp.concatenate([att_ref[head, block] for head in range(heads)], axis=0)
            for block in range(blocks)
        ],
        axis=1,
    )


def mixed_kernel(att_ref, wo_ref, mixed_ref):
    attended = attended_columns(att_ref).T
    mixed_ref[...] = dot(attended, wo_ref[...], ((1,), (0,))).astype(jnp.bfloat16)


def unpack_kernel(in_ref, gq_ref, gk_ref, gv_ref):
    blocks = in_ref.shape[1]
    low = lax.broadcasted_iota(jnp.int32, (BLOCK_ROWS, LANES), 1) < HEAD_WIDTH
    for block in range(blocks):
        rows = slice(block * BLOCK_ROWS, (block + 1) * BLOCK_ROWS)
        for head in range(0, HEADS, 2):
            columns = slice(head * HEAD_WIDTH, (head + 2) * HEAD_WIDTH)
            flat = jnp.concatenate([in_ref[head + i, block, :HEAD_WIDTH] for i in range(2)], axis=0)
            gq_ref[rows, columns] = flat.T
            one, two = (in_ref[head + i, block, HEAD_WIDTH:] for i in range(2))
            gk_ref[rows, columns] = jnp.concatenate(
                [one[:, :HEAD_WIDTH], two[:, :HEAD_WIDTH]], axis=1
            )
            gv_ref[rows, columns] = jnp.concatenate(
                [one[:, HEAD_WIDTH:], two[:, HEAD_WIDTH:]], axis=1
            )


def by_falling_count(counts):
    index = jnp.arange(counts.shape[0], dtype=jnp.int32)
    place = -counts * counts.shape[0] + index
    rank = jnp.sum((place[None, :] < place[:, None]).astype(jnp.int32), axis=1)
    return jnp.sum(jnp.where(rank[None, :] == index[:, None], index[None, :], 0), axis=1)


def exchange(array):
    return lax.all_to_all(array, "seq", split_axis=0, concat_axis=0, tiled=True)


def local(queries, keys, values, upstream, w_out, key_blocks, block_counts):
    local_rows, width = queries.shape[1:]
    seq_size, dp_size = lax.axis_size("seq"), lax.axis_size("dp")
    lists, counts = key_blocks[0], block_counts[0]
    blocks, listed = lists.shape
    near_blocks = local_rows // BLOCK_ROWS
    up_rows = upstream[0]
    bf16, f32 = jnp.bfloat16, jnp.float32
    shape = jax.ShapeDtypeStruct
    smem, vmem = SMEM_SPEC, VMEM_SPEC

    packed = exchange(pack(queries[0], keys[0], values[0], up_rows, w_out))
    half = width // 2
    core = (lax.axis_index("dp") % 2).reshape(1).astype(jnp.int32)
    other_core = [(i, i + 1 - 2 * (i % 2)) for i in range(dp_size)]
    own_up, send_up = call(
        split_columns_kernel,
        "split_columns",
        [shape((local_rows, half), bf16)] * 2,
        [smem, vmem],
        flops=10**8,
    )(core, up_rows)
    other_up = lax.ppermute(send_up, "dp", other_core)
    packed, own_up, other_up = lax.optimization_barrier((packed, own_up, other_up))
    packed = packed.reshape(blocks, 2 * BLOCK_ROWS, LANES)
    lists, counts, order = lax.optimization_barrier((lists, counts, by_falling_count(counts)))
    listing = (lists, counts, order)
    turned = pltpu.VMEM((blocks, HEAD_WIDTH, BLOCK_ROWS), bf16)
    acc = (blocks, BLOCK_ROWS, LANES)
    half_turned = shape((blocks, HEAD_WIDTH, BLOCK_ROWS), bf16)

    attended, stats = call(
        forward_kernel,
        "forward",
        [half_turned, shape((blocks, 8, BLOCK_ROWS), f32)],
        [smem] * 3 + [vmem],
        [turned] + [pltpu.VMEM((listed * BLOCK_ROWS, BLOCK_ROWS), f32)] * FORWARD_TILE,
        flops=10 * 10**9,
    )(*listing, packed)

    attended = exchange(attended.reshape(seq_size, near_blocks, HEAD_WIDTH, BLOCK_ROWS))
    gq_first, acc_first, token = call(
        functools.partial(backward_kernel, (0, FIRST_TILES), True),
        "backward_first",
        [half_turned, shape(acc, f32), shape((8, LANES), f32)],
        [smem] * 3 + [vmem] * 2,
        [turned, pltpu.VMEM(acc, f32), pltpu.SemaphoreType.DMA((1,))],
        flops=10 * 10**9,
        vmem=61,
        out_specs=[vmem, HBM_SPEC, vmem],
    )(*listing, packed, stats)

    attended, token = lax.optimization_barrier((attended, token))
    (chip_sum,) = call(
        weight_grad_kernel,
        "weight_grad",
        [shape((width, half), bf16)],
        [vmem] * 5,
        flops=10**9,
    )(attended, lax.ppermute(attended, "dp", other_core), own_up, other_up, token)

    chip_sum, stats = lax.optimization_barrier((chip_sum, stats))
    parts = exchange(chip_sum.reshape(seq_size, width // seq_size, half))
    out_shape = (blocks, HEAD_WIDTH + BLOCK_ROWS, LANES)
    outgoing, token = call(
        functools.partial(backward_kernel, (FIRST_TILES, blocks // BACKWARD_TILE), False),
        "backward_second",
        [shape(out_shape, bf16), shape((8, LANES), f32)],
        [smem] * 3 + [vmem] * 3 + [HBM_SPEC],
        [
            turned,
            pltpu.VMEM(acc, f32),
            pltpu.VMEM(acc, f32),
            pltpu.VMEM(out_shape, bf16),
            pltpu.SemaphoreType.DMA((1 + blocks // 4,)),
        ],
        flops=15 * 10**9,
        vmem=61,
        out_specs=[HBM_SPEC, vmem],
    )(*listing, packed, stats, gq_first, acc_first)

    parts, _ = lax.optimization_barrier((parts, token))
    incoming = exchange(
        outgoing.reshape(seq_size, near_blocks, HEAD_WIDTH + BLOCK_ROWS, LANES)
    )
    grad_wo = jnp.sum(parts.astype(f32), axis=0)
    chips = dp_size // 2
    chip = lax.axis_index("dp") // 2
    apart = chips // 2
    while apart:
        below, above = jnp.split(grad_wo, 2, axis=1)
        upper = (chip // apart) % 2 == 1
        opposite = [(i, 2 * ((i // 2) ^ apart) + i % 2) for i in range(dp_size)]
        received = lax.ppermute(jnp.where(upper, below, above).astype(bf16), "dp", opposite)
        grad_wo = jnp.where(upper, above, below) + received.astype(f32)
        apart //= 2
    grad_wo = grad_wo * (1.0 / math.sqrt(dp_size * local_rows * seq_size))

    rows = shape((local_rows, width), bf16)
    (mixed,) = call(mixed_kernel, "mixed", [rows], [vmem] * 2, flops=10**9)(attended, w_out)
    gq, gk, gv = call(unpack_kernel, "unpack", [rows] * 3, [vmem])(incoming)
    full_shape = (1, local_rows, width)
    return (
        mixed.reshape(full_shape),
        gq.reshape(full_shape),
        gk.reshape(full_shape),
        gv.reshape(full_shape),
        grad_wo,
    )


def solution(mesh):
    nodes = P("dp", "seq", None)
    return jax.shard_map(
        local,
        mesh=mesh,
        in_specs=(nodes, nodes, nodes, nodes, P(), P("dp", None, None), P("dp", None)),
        out_specs=(nodes, nodes, nodes, nodes, P("seq", "dp")),
        check_vma=False,
    )
```

```python
import functools
import math

import jax
import jax.numpy as jnp
from jax import lax
from jax.experimental import pallas as pl
from jax.experimental.pallas import tpu as pltpu
from jax.sharding import PartitionSpec as P

HEADS = 16
HEAD_WIDTH = 64
BLOCK_ROWS = 128
LANES = 2 * HEAD_WIDTH
FORWARD_TILE = 4
BACKWARD_TILE = 2
SLOT_STEP = 2
FIRST_TILES = 4
MASKED = -1e30
SCORE_SCALE = 1.0 / math.sqrt(HEAD_WIDTH)
EXP2_SCALE = SCORE_SCALE * math.log2(math.e)

HBM_SPEC = pl.BlockSpec(memory_space=pltpu.HBM)
VMEM_SPEC = pl.BlockSpec(memory_space=pltpu.VMEM)
SMEM_SPEC = pl.BlockSpec(memory_space=pltpu.SMEM)


def dot(left, right, contract):
    return lax.dot_general(
        left, right, (contract, ((), ())), preferred_element_type=jnp.float32
    )


def call(kernel, name, outs, in_specs, scratch=(), flops=0, out_specs=None, vmem=24):
    return pl.pallas_call(
        kernel,
        out_shape=outs,
        in_specs=in_specs,
        out_specs=out_specs or [VMEM_SPEC] * len(outs),
        scratch_shapes=list(scratch),
        compiler_params=pltpu.CompilerParams(vmem_limit_bytes=vmem * 2**20),
        cost_estimate=pl.CostEstimate(flops=flops, bytes_accessed=4 * 2**20, transcendentals=0),
        name=name,
    )


def sort_by_falling_count(count_ref, order_ref, place_ref):
    places = place_ref.shape[0]
    for i in range(places):
        place_ref[i] = 0

    def tally(block, _):
        count = count_ref[block]
        place_ref[count] = place_ref[count] + 1
        return 0

    lax.fori_loop(0, count_ref.shape[0], tally, 0)
    before = jnp.int32(0)
    for i in reversed(range(places)):
        here = place_ref[i]
        place_ref[i] = before
        before = before + here

    def put(block, _):
        count = count_ref[block]
        place = place_ref[count]
        order_ref[place] = block
        place_ref[count] = place + 1
        return 0

    lax.fori_loop(0, count_ref.shape[0], put, 0)


def pack_kernel(
    count_ref, query_ref, key_ref, value_ref, up_ref, wo_ref, out_ref, order_ref, place_ref
):
    @pl.when(pl.program_id(0) == 0)
    def _():
        sort_by_falling_count(count_ref, order_ref, place_ref)

    grads = dot(up_ref[...], wo_ref[...], ((1,), (1,))).astype(jnp.bfloat16)
    heads_here = out_ref.shape[0]
    for head in range(heads_here):
        columns = slice(head * HEAD_WIDTH, (head + 1) * HEAD_WIDTH)
        kv = jnp.concatenate([key_ref[:, columns], value_ref[:, columns]], axis=1)
        qg = jnp.concatenate([query_ref[:, columns], grads[:, columns]], axis=1)
        for block in range(out_ref.shape[1]):
            rows = slice(block * BLOCK_ROWS, (block + 1) * BLOCK_ROWS)
            out_ref[head, block, :BLOCK_ROWS] = kv[rows]
            out_ref[head, block, BLOCK_ROWS:] = qg[rows]


def pack(counts, listed, queries, keys, values, up_rows, w_out):
    rows, width = queries.shape
    blocks = rows // BLOCK_ROWS
    steps = 2
    columns = width // steps
    part = pl.BlockSpec((rows, columns), lambda i: (0, i))
    return pl.pallas_call(
        pack_kernel,
        grid=(steps,),
        out_shape=[
            jax.ShapeDtypeStruct((HEADS, blocks, 2 * BLOCK_ROWS, LANES), jnp.bfloat16),
            jax.ShapeDtypeStruct(counts.shape, jnp.int32),
        ],
        in_specs=[
            SMEM_SPEC,
            part,
            part,
            part,
            pl.BlockSpec((rows, width), lambda i: (0, 0)),
            pl.BlockSpec((columns, width), lambda i: (i, 0)),
        ],
        out_specs=[
            pl.BlockSpec((HEADS // steps, blocks, 2 * BLOCK_ROWS, LANES), lambda i: (i, 0, 0, 0)),
            SMEM_SPEC,
        ],
        scratch_shapes=[pltpu.SMEM((listed + 1,), jnp.int32)],
        compiler_params=pltpu.CompilerParams(vmem_limit_bytes=60 * 2**20),
        name="pack",
    )(counts, queries, keys, values, up_rows, w_out)


def for_tiles(tiles, tile_blocks, listed, order_ref, count_ref, process):
    def one_tile(tile, _):
        members = [order_ref[tile * tile_blocks + i] for i in range(tile_blocks)]
        steps = (count_ref[members[0]] + SLOT_STEP - 1) // SLOT_STEP
        sizes = range(SLOT_STEP, listed + 1, SLOT_STEP)
        lax.switch(steps - 1, [functools.partial(process, members, size) for size in sizes])
        return 0

    lax.fori_loop(*tiles, one_tile, 0)


def by_fours(blocks, body):
    def four(index, _):
        for unit in range(4):
            body(4 * index + unit)
        return 0

    lax.fori_loop(0, blocks // 4, four, 0)


def forward_kernel(list_ref, count_ref, order_ref, in_ref, att_ref, stat_ref, turned, *score_bufs):
    listed, blocks = list_ref.shape
    low = lax.broadcasted_iota(jnp.int32, (LANES, BLOCK_ROWS), 0) < HEAD_WIDTH

    def turn(block):
        turned[block] = in_ref[block, :BLOCK_ROWS].T[HEAD_WIDTH:]

    by_fours(blocks, turn)

    def process(members, slots):
        qg_turned = [in_ref[block, BLOCK_ROWS:].T for block in members]
        queries = [jnp.where(low, array, jnp.zeros_like(array)) for array in qg_turned]
        near = [[list_ref[slot, block] for slot in range(slots)] for block in members]
        highest = []
        for i, block in enumerate(members):
            rows = jnp.concatenate([in_ref[key, :BLOCK_ROWS] for key in near[i]], axis=0)
            scores = dot(rows, queries[i], ((1,), (0,)))
            top = jnp.full((8, BLOCK_ROWS), MASKED, jnp.float32)
            for slot in range(slots):
                here = slice(slot * BLOCK_ROWS, (slot + 1) * BLOCK_ROWS)
                part = jnp.where(slot < count_ref[block], scores[here], MASKED)
                score_bufs[i][here] = part
                top = jnp.maximum(top, jnp.max(part.reshape(-1, 8, BLOCK_ROWS), axis=0))
            highest.append(jnp.max(top, axis=0, keepdims=True))
        for i, block in enumerate(members):
            part = score_bufs[i][: slots * BLOCK_ROWS]
            raised = jnp.exp2((part - highest[i]) * EXP2_SCALE)
            total = jnp.sum(raised, axis=0, keepdims=True)
            flat = jnp.concatenate([turned[key] for key in near[i]], axis=1)
            sums = dot(flat, raised.astype(jnp.bfloat16), ((1,), (0,)))
            attended = (sums * (1.0 / total)).astype(jnp.bfloat16)
            att_ref[block] = attended
            grads = qg_turned[i][HEAD_WIDTH:].astype(jnp.float32)
            delta = jnp.sum(attended.astype(jnp.float32) * grads, axis=0, keepdims=True)
            stat_ref[block, 0:1] = highest[i] + jnp.log2(total) * (1.0 / EXP2_SCALE)
            stat_ref[block, 1:2] = delta

    for_tiles(
        (0, blocks // FORWARD_TILE), FORWARD_TILE, listed, order_ref, count_ref, process
    )


def backward_kernel(tiles, first, list_ref, count_ref, order_ref, in_ref, stat_ref, *refs):
    if first:
        out_ref, token_ref, turned, acc_ref = refs
    else:
        part_hbm, out_hbm, token_ref, turned, acc_ref, out_ref, sems = refs
        fetch = pltpu.make_async_copy(part_hbm, out_ref, sems.at[0])
        fetch.start()
    token_ref[...] = jnp.zeros_like(token_ref)
    listed, blocks = list_ref.shape
    low_lanes = lax.broadcasted_iota(jnp.int32, (BLOCK_ROWS, LANES), 1) < HEAD_WIDTH
    low_rows = lax.broadcasted_iota(jnp.int32, (LANES, BLOCK_ROWS), 0) < HEAD_WIDTH

    def prepare(block):
        turned[block] = in_ref[block, :BLOCK_ROWS].T[:HEAD_WIDTH]
        acc_ref[block] = jnp.zeros((BLOCK_ROWS, LANES), jnp.float32)

    by_fours(blocks, prepare)
    if not first:
        fetch.wait()

    def process(members, slots):
        for block in members:
            qg = in_ref[block, BLOCK_ROWS:]
            flat = qg.T
            zero = jnp.zeros_like(qg)
            across = jnp.concatenate(
                [jnp.where(low_rows, flat, zero), jnp.where(low_rows, zero, flat)], axis=1
            )
            down = jnp.concatenate(
                [jnp.where(low_lanes, qg, zero), jnp.where(low_lanes, zero, qg)], axis=0
            )
            top, delta = stat_ref[block, 0:1], stat_ref[block, 1:2]
            near = [list_ref[slot, block] for slot in range(slots)]
            rows = jnp.concatenate([in_ref[key, :BLOCK_ROWS] for key in near], axis=0)
            both = dot(rows, across, ((1,), (0,)))
            joined = []
            for slot in range(slots):
                part = both[slot * BLOCK_ROWS : (slot + 1) * BLOCK_ROWS]
                probability = jnp.exp2((part[:, :BLOCK_ROWS] - top) * EXP2_SCALE)
                probability = jnp.where(slot < count_ref[block], probability, 0.0)
                logits = probability * (part[:, BLOCK_ROWS:] - delta)
                joined.append(
                    jnp.concatenate(
                        [logits.astype(jnp.bfloat16), probability.astype(jnp.bfloat16)], axis=1
                    )
                )
            joined = jnp.concatenate(joined, axis=0)
            key_terms = dot(joined, down, ((1,), (0,)))
            for slot, key in enumerate(near):
                acc_ref[key] += key_terms[slot * BLOCK_ROWS : (slot + 1) * BLOCK_ROWS]
            flat = jnp.concatenate([turned[key] for key in near], axis=1)
            grads = dot(flat, joined[:, :BLOCK_ROWS], ((1,), (0,)))
            out_ref[block, :HEAD_WIDTH] = (grads * SCORE_SCALE).astype(jnp.bfloat16)

    for_tiles(tiles, BACKWARD_TILE, listed, order_ref, count_ref, process)
    if first:

        def keep(block):
            out_ref[block, HEAD_WIDTH:] = acc_ref[block].astype(jnp.bfloat16)

        by_fours(blocks, keep)
        return
    scale = jnp.where(low_lanes, SCORE_SCALE, 1.0)

    def stores(chunk):
        here = pl.ds(4 * chunk, 4)
        return pltpu.make_async_copy(out_ref.at[here], out_hbm.at[here], sems.at[1 + chunk])

    for chunk in range(blocks // 4):
        for block in range(4 * chunk, 4 * chunk + 4):
            total = acc_ref[block] + out_ref[block, HEAD_WIDTH:].astype(jnp.float32)
            out_ref[block, HEAD_WIDTH:] = (total * scale).astype(jnp.bfloat16)
        stores(chunk).start()
    for chunk in range(blocks // 4):
        stores(chunk).wait()


def split_columns_kernel(core_ref, up_ref, keep_ref, send_ref):
    pieces = up_ref.shape[1] // HEAD_WIDTH

    def every_other(start):
        return jnp.concatenate(
            [up_ref[:, i * HEAD_WIDTH : (i + 1) * HEAD_WIDTH] for i in range(start, pieces, 2)],
            axis=1,
        )

    even, odd = every_other(0), every_other(1)
    first = core_ref[0] == 0
    keep_ref[...] = jnp.where(first, even, odd)
    send_ref[...] = jnp.where(first, odd, even)


def weight_grad_kernel(own_att_ref, other_att_ref, own_up_ref, other_up_ref, token_ref, out_ref):
    attended = jnp.concatenate(
        [attended_columns(own_att_ref), attended_columns(other_att_ref)], axis=1
    )
    up_rows = jnp.concatenate([own_up_ref[...], other_up_ref[...]], axis=0)
    out_ref[...] = dot(attended, up_rows, ((1,), (0,))).astype(jnp.bfloat16)


def attended_columns(att_ref):
    heads, blocks = att_ref.shape[:2]
    return jnp.concatenate(
        [
            jnp.concatenate([att_ref[head, block] for head in range(heads)], axis=0)
            for block in range(blocks)
        ],
        axis=1,
    )


def mixed_kernel(att_ref, wo_ref, mixed_ref):
    attended = attended_columns(att_ref).T
    mixed_ref[...] = dot(attended, wo_ref[...], ((1,), (0,))).astype(jnp.bfloat16)


def unpack_kernel(in_ref, gq_ref, gk_ref, gv_ref):
    blocks = in_ref.shape[1]
    low = lax.broadcasted_iota(jnp.int32, (BLOCK_ROWS, LANES), 1) < HEAD_WIDTH
    for block in range(blocks):
        rows = slice(block * BLOCK_ROWS, (block + 1) * BLOCK_ROWS)
        for head in range(0, HEADS, 2):
            columns = slice(head * HEAD_WIDTH, (head + 2) * HEAD_WIDTH)
            flat = jnp.concatenate([in_ref[head + i, block, :HEAD_WIDTH] for i in range(2)], axis=0)
            gq_ref[rows, columns] = flat.T
            one, two = (in_ref[head + i, block, HEAD_WIDTH:] for i in range(2))
            gk_ref[rows, columns] = jnp.concatenate(
                [one[:, :HEAD_WIDTH], two[:, :HEAD_WIDTH]], axis=1
            )
            gv_ref[rows, columns] = jnp.concatenate(
                [one[:, HEAD_WIDTH:], two[:, HEAD_WIDTH:]], axis=1
            )


def exchange(array):
    return lax.all_to_all(array, "seq", split_axis=0, concat_axis=0, tiled=True)


def local(queries, keys, values, upstream, w_out, key_blocks, block_counts):
    local_rows, width = queries.shape[1:]
    seq_size, dp_size = lax.axis_size("seq"), lax.axis_size("dp")
    lists, counts = key_blocks[0].T, block_counts[0]
    listed, blocks = lists.shape
    near_blocks = local_rows // BLOCK_ROWS
    up_rows = upstream[0]
    bf16, f32 = jnp.bfloat16, jnp.float32
    shape = jax.ShapeDtypeStruct
    smem, vmem = SMEM_SPEC, VMEM_SPEC

    packed, order = pack(counts, listed, queries[0], keys[0], values[0], up_rows, w_out)
    packed = exchange(packed)
    packed, up_rows = lax.optimization_barrier((packed, up_rows))
    half = width // 2
    core = (lax.axis_index("dp") % 2).reshape(1).astype(jnp.int32)
    other_core = [(i, i + 1 - 2 * (i % 2)) for i in range(dp_size)]
    own_up, send_up = call(
        split_columns_kernel,
        "split_columns",
        [shape((local_rows, half), bf16)] * 2,
        [smem, vmem],
        flops=10**8,
    )(core, up_rows)
    other_up = lax.ppermute(send_up, "dp", other_core)
    packed = packed.reshape(blocks, 2 * BLOCK_ROWS, LANES)
    listing = (lists, counts, order)
    turned = pltpu.VMEM((blocks, HEAD_WIDTH, BLOCK_ROWS), bf16)
    acc = (blocks, BLOCK_ROWS, LANES)
    half_turned = shape((blocks, HEAD_WIDTH, BLOCK_ROWS), bf16)

    attended, stats = call(
        forward_kernel,
        "forward",
        [half_turned, shape((blocks, 8, BLOCK_ROWS), f32)],
        [smem] * 3 + [vmem],
        [turned] + [pltpu.VMEM((listed * BLOCK_ROWS, BLOCK_ROWS), f32)] * FORWARD_TILE,
        flops=10 * 10**9,
    )(*listing, packed)

    attended = exchange(attended.reshape(seq_size, near_blocks, HEAD_WIDTH, BLOCK_ROWS))
    out_shape = (blocks, HEAD_WIDTH + BLOCK_ROWS, LANES)
    outgoing, token = call(
        functools.partial(backward_kernel, (0, FIRST_TILES), True),
        "backward_first",
        [shape(out_shape, bf16), shape((8, LANES), f32)],
        [smem] * 3 + [vmem] * 2,
        [turned, pltpu.VMEM(acc, f32)],
        flops=10 * 10**9,
    )(*listing, packed, stats)

    attended, token = lax.optimization_barrier((attended, token))
    (chip_sum,) = call(
        weight_grad_kernel,
        "weight_grad",
        [shape((width, half), bf16)],
        [vmem] * 5,
        flops=10**9,
    )(attended, lax.ppermute(attended, "dp", other_core), own_up, other_up, token)

    chip_sum, stats = lax.optimization_barrier((chip_sum, stats))
    parts = exchange(chip_sum.reshape(seq_size, width // seq_size, half))
    outgoing, token = call(
        functools.partial(backward_kernel, (FIRST_TILES, blocks // BACKWARD_TILE), False),
        "backward_second",
        [shape(out_shape, bf16), shape((8, LANES), f32)],
        [smem] * 3 + [vmem] * 2 + [HBM_SPEC],
        [
            turned,
            pltpu.VMEM(acc, f32),
            pltpu.VMEM(out_shape, bf16),
            pltpu.SemaphoreType.DMA((1 + blocks // 4,)),
        ],
        flops=15 * 10**9,
        vmem=61,
        out_specs=[HBM_SPEC, vmem],
    )(*listing, packed, stats, outgoing)

    parts, _ = lax.optimization_barrier((parts, token))
    incoming = exchange(
        outgoing.reshape(seq_size, near_blocks, HEAD_WIDTH + BLOCK_ROWS, LANES)
    )
    grad_wo = jnp.sum(parts.astype(f32), axis=0)
    chips = dp_size // 2
    chip = lax.axis_index("dp") // 2
    apart = chips // 2
    while apart:
        below, above = jnp.split(grad_wo, 2, axis=1)
        upper = (chip // apart) % 2 == 1
        opposite = [(i, 2 * ((i // 2) ^ apart) + i % 2) for i in range(dp_size)]
        received = lax.ppermute(jnp.where(upper, below, above).astype(bf16), "dp", opposite)
        grad_wo = jnp.where(upper, above, below) + received.astype(f32)
        apart //= 2
    grad_wo = grad_wo * (1.0 / math.sqrt(dp_size * local_rows * seq_size))

    rows = shape((local_rows, width), bf16)
    (mixed,) = call(mixed_kernel, "mixed", [rows], [vmem] * 2, flops=10**9)(attended, w_out)
    gq, gk, gv = call(unpack_kernel, "unpack", [rows] * 3, [vmem])(incoming)
    full_shape = (1, local_rows, width)
    return (
        mixed.reshape(full_shape),
        gq.reshape(full_shape),
        gk.reshape(full_shape),
        gv.reshape(full_shape),
        grad_wo,
    )


def solution(mesh):
    nodes = P("dp", "seq", None)
    return jax.shard_map(
        local,
        mesh=mesh,
        in_specs=(nodes, nodes, nodes, nodes, P(), P("dp", None, None), P("dp", None)),
        out_specs=(nodes, nodes, nodes, nodes, P("seq", "dp")),
        check_vma=False,
    )
```

```python
import functools
import math

import jax
import jax.numpy as jnp
from jax import lax
from jax.experimental import pallas as pl
from jax.experimental.pallas import tpu as pltpu
from jax.sharding import PartitionSpec as P

HEADS = 16
HEAD_WIDTH = 64
BLOCK_ROWS = 128
LANES = 2 * HEAD_WIDTH
FORWARD_TILE = 4
FIRST_BACKWARD_TILE = 2
SECOND_BACKWARD_TILE = 4
SLOT_STEP = 2
FIRST_BLOCKS = 8
MASKED = -1e30
SCORE_SCALE = 1.0 / math.sqrt(HEAD_WIDTH)
EXP2_SCALE = SCORE_SCALE * math.log2(math.e)

HBM_SPEC = pl.BlockSpec(memory_space=pltpu.HBM)
VMEM_SPEC = pl.BlockSpec(memory_space=pltpu.VMEM)
SMEM_SPEC = pl.BlockSpec(memory_space=pltpu.SMEM)


def dot(left, right, contract):
    return lax.dot_general(
        left, right, (contract, ((), ())), preferred_element_type=jnp.float32
    )


def call(kernel, name, outs, in_specs, scratch=(), flops=0, out_specs=None, vmem=24):
    return pl.pallas_call(
        kernel,
        out_shape=outs,
        in_specs=in_specs,
        out_specs=out_specs or [VMEM_SPEC] * len(outs),
        scratch_shapes=list(scratch),
        compiler_params=pltpu.CompilerParams(vmem_limit_bytes=vmem * 2**20),
        cost_estimate=pl.CostEstimate(flops=flops, bytes_accessed=4 * 2**20, transcendentals=0),
        name=name,
    )


def sort_by_falling_count(count_ref, order_ref, place_ref):
    places = place_ref.shape[0]
    for i in range(places):
        place_ref[i] = 0

    def tally(block, _):
        count = count_ref[block]
        place_ref[count] = place_ref[count] + 1
        return 0

    lax.fori_loop(0, count_ref.shape[0], tally, 0)
    before = jnp.int32(0)
    for i in reversed(range(places)):
        here = place_ref[i]
        place_ref[i] = before
        before = before + here

    def put(block, _):
        count = count_ref[block]
        place = place_ref[count]
        order_ref[place] = block
        place_ref[count] = place + 1
        return 0

    lax.fori_loop(0, count_ref.shape[0], put, 0)


def pack_kernel(
    count_ref, query_ref, key_ref, value_ref, up_ref, wo_ref, out_ref, order_ref, place_ref
):
    @pl.when(pl.program_id(0) == 0)
    def _():
        sort_by_falling_count(count_ref, order_ref, place_ref)

    grads = dot(up_ref[...], wo_ref[...], ((1,), (1,))).astype(jnp.bfloat16)
    heads_here = out_ref.shape[0]
    for head in range(heads_here):
        columns = slice(head * HEAD_WIDTH, (head + 1) * HEAD_WIDTH)
        kv = jnp.concatenate([key_ref[:, columns], value_ref[:, columns]], axis=1)
        qg = jnp.concatenate([query_ref[:, columns], grads[:, columns]], axis=1)
        for block in range(out_ref.shape[1]):
            rows = slice(block * BLOCK_ROWS, (block + 1) * BLOCK_ROWS)
            out_ref[head, block, :BLOCK_ROWS] = kv[rows]
            out_ref[head, block, BLOCK_ROWS:] = qg[rows]


def pack(counts, listed, queries, keys, values, up_rows, w_out):
    rows, width = queries.shape
    blocks = rows // BLOCK_ROWS
    steps = 2
    columns = width // steps
    part = pl.BlockSpec((rows, columns), lambda i: (0, i))
    return pl.pallas_call(
        pack_kernel,
        grid=(steps,),
        out_shape=[
            jax.ShapeDtypeStruct((HEADS, blocks, 2 * BLOCK_ROWS, LANES), jnp.bfloat16),
            jax.ShapeDtypeStruct(counts.shape, jnp.int32),
        ],
        in_specs=[
            SMEM_SPEC,
            part,
            part,
            part,
            pl.BlockSpec((rows, width), lambda i: (0, 0)),
            pl.BlockSpec((columns, width), lambda i: (i, 0)),
        ],
        out_specs=[
            pl.BlockSpec((HEADS // steps, blocks, 2 * BLOCK_ROWS, LANES), lambda i: (i, 0, 0, 0)),
            SMEM_SPEC,
        ],
        scratch_shapes=[pltpu.SMEM((listed + 1,), jnp.int32)],
        compiler_params=pltpu.CompilerParams(vmem_limit_bytes=60 * 2**20),
        name="pack",
    )(counts, queries, keys, values, up_rows, w_out)


def for_tiles(tiles, tile_blocks, listed, order_ref, count_ref, process):
    def one_tile(tile, _):
        members = [order_ref[tile * tile_blocks + i] for i in range(tile_blocks)]
        steps = (count_ref[members[0]] + SLOT_STEP - 1) // SLOT_STEP
        sizes = range(SLOT_STEP, listed + 1, SLOT_STEP)
        lax.switch(steps - 1, [functools.partial(process, members, size) for size in sizes])
        return 0

    lax.fori_loop(*tiles, one_tile, 0)


def by_fours(blocks, body):
    def four(index, _):
        for unit in range(4):
            body(4 * index + unit)
        return 0

    lax.fori_loop(0, blocks // 4, four, 0)


def forward_kernel(list_ref, count_ref, order_ref, in_ref, att_ref, stat_ref, turned, *score_bufs):
    listed, blocks = list_ref.shape
    low = lax.broadcasted_iota(jnp.int32, (LANES, BLOCK_ROWS), 0) < HEAD_WIDTH

    def turn(block):
        turned[block] = in_ref[block, :BLOCK_ROWS].T[HEAD_WIDTH:]

    by_fours(blocks, turn)

    def process(members, slots):
        qg_turned = [in_ref[block, BLOCK_ROWS:].T for block in members]
        queries = [jnp.where(low, array, jnp.zeros_like(array)) for array in qg_turned]
        near = [[list_ref[slot, block] for slot in range(slots)] for block in members]
        highest = []
        for i, block in enumerate(members):
            rows = jnp.concatenate([in_ref[key, :BLOCK_ROWS] for key in near[i]], axis=0)
            scores = dot(rows, queries[i], ((1,), (0,)))
            top = jnp.full((8, BLOCK_ROWS), MASKED, jnp.float32)
            for slot in range(slots):
                here = slice(slot * BLOCK_ROWS, (slot + 1) * BLOCK_ROWS)
                part = jnp.where(slot < count_ref[block], scores[here], MASKED)
                score_bufs[i][here] = part
                top = jnp.maximum(top, jnp.max(part.reshape(-1, 8, BLOCK_ROWS), axis=0))
            highest.append(jnp.max(top, axis=0, keepdims=True))
        for i, block in enumerate(members):
            part = score_bufs[i][: slots * BLOCK_ROWS]
            raised = jnp.exp2((part - highest[i]) * EXP2_SCALE)
            total = jnp.sum(raised, axis=0, keepdims=True)
            flat = jnp.concatenate([turned[key] for key in near[i]], axis=1)
            sums = dot(flat, raised.astype(jnp.bfloat16), ((1,), (0,)))
            attended = (sums * (1.0 / total)).astype(jnp.bfloat16)
            att_ref[block] = attended
            grads = qg_turned[i][HEAD_WIDTH:].astype(jnp.float32)
            delta = jnp.sum(attended.astype(jnp.float32) * grads, axis=0, keepdims=True)
            stat_ref[block, 0:1] = highest[i] + jnp.log2(total) * (1.0 / EXP2_SCALE)
            stat_ref[block, 1:2] = delta

    for_tiles(
        (0, blocks // FORWARD_TILE), FORWARD_TILE, listed, order_ref, count_ref, process
    )


def backward_kernel(tiles, first, list_ref, count_ref, order_ref, in_ref, stat_ref, *refs):
    if first:
        out_ref, token_ref, turned, acc_ref = refs
    else:
        part_hbm, out_hbm, token_ref, turned, acc_ref, out_ref, sems = refs
        fetch = pltpu.make_async_copy(part_hbm, out_ref, sems.at[0])
        fetch.start()
    token_ref[...] = jnp.zeros_like(token_ref)
    listed, blocks = list_ref.shape
    low_lanes = lax.broadcasted_iota(jnp.int32, (BLOCK_ROWS, LANES), 1) < HEAD_WIDTH
    low_rows = lax.broadcasted_iota(jnp.int32, (LANES, BLOCK_ROWS), 0) < HEAD_WIDTH

    def prepare(block):
        turned[block] = in_ref[block, :BLOCK_ROWS].T[:HEAD_WIDTH]
        acc_ref[block] = jnp.zeros((BLOCK_ROWS, LANES), jnp.float32)

    by_fours(blocks, prepare)
    if not first:
        fetch.wait()

    def process(members, slots):
        for block in members:
            qg = in_ref[block, BLOCK_ROWS:]
            flat = qg.T
            zero = jnp.zeros_like(qg)
            across = jnp.concatenate(
                [jnp.where(low_rows, flat, zero), jnp.where(low_rows, zero, flat)], axis=1
            )
            down = jnp.concatenate(
                [jnp.where(low_lanes, qg, zero), jnp.where(low_lanes, zero, qg)], axis=0
            )
            top, delta = stat_ref[block, 0:1], stat_ref[block, 1:2]
            near = [list_ref[slot, block] for slot in range(slots)]
            rows = jnp.concatenate([in_ref[key, :BLOCK_ROWS] for key in near], axis=0)
            both = dot(rows, across, ((1,), (0,)))
            joined = []
            for slot in range(slots):
                part = both[slot * BLOCK_ROWS : (slot + 1) * BLOCK_ROWS]
                probability = jnp.exp2((part[:, :BLOCK_ROWS] - top) * EXP2_SCALE)
                probability = jnp.where(slot < count_ref[block], probability, 0.0)
                logits = probability * (part[:, BLOCK_ROWS:] - delta)
                joined.append(
                    jnp.concatenate(
                        [logits.astype(jnp.bfloat16), probability.astype(jnp.bfloat16)], axis=1
                    )
                )
            joined = jnp.concatenate(joined, axis=0)
            key_terms = dot(joined, down, ((1,), (0,)))
            for slot, key in enumerate(near):
                acc_ref[key] += key_terms[slot * BLOCK_ROWS : (slot + 1) * BLOCK_ROWS]
            flat = jnp.concatenate([turned[key] for key in near], axis=1)
            grads = dot(flat, joined[:, :BLOCK_ROWS], ((1,), (0,)))
            out_ref[block, :HEAD_WIDTH] = (grads * SCORE_SCALE).astype(jnp.bfloat16)

    for_tiles(tiles, FIRST_BACKWARD_TILE if first else SECOND_BACKWARD_TILE, listed, order_ref, count_ref, process)
    if first:

        def keep(block):
            out_ref[block, HEAD_WIDTH:] = acc_ref[block].astype(jnp.bfloat16)

        by_fours(blocks, keep)
        return
    scale = jnp.where(low_lanes, SCORE_SCALE, 1.0)

    def stores(chunk):
        here = pl.ds(4 * chunk, 4)
        return pltpu.make_async_copy(out_ref.at[here], out_hbm.at[here], sems.at[1 + chunk])

    for chunk in range(blocks // 4):
        for block in range(4 * chunk, 4 * chunk + 4):
            total = acc_ref[block] + out_ref[block, HEAD_WIDTH:].astype(jnp.float32)
            out_ref[block, HEAD_WIDTH:] = (total * scale).astype(jnp.bfloat16)
        stores(chunk).start()
    for chunk in range(blocks // 4):
        stores(chunk).wait()


def split_columns_kernel(core_ref, up_ref, keep_ref, send_ref):
    pieces = up_ref.shape[1] // HEAD_WIDTH

    def every_other(start):
        return jnp.concatenate(
            [up_ref[:, i * HEAD_WIDTH : (i + 1) * HEAD_WIDTH] for i in range(start, pieces, 2)],
            axis=1,
        )

    even, odd = every_other(0), every_other(1)
    first = core_ref[0] == 0
    keep_ref[...] = jnp.where(first, even, odd)
    send_ref[...] = jnp.where(first, odd, even)


def weight_grad_kernel(own_att_ref, other_att_ref, own_up_ref, other_up_ref, token_ref, out_ref):
    attended = jnp.concatenate(
        [attended_columns(own_att_ref), attended_columns(other_att_ref)], axis=1
    )
    up_rows = jnp.concatenate([own_up_ref[...], other_up_ref[...]], axis=0)
    out_ref[...] = dot(attended, up_rows, ((1,), (0,))).astype(jnp.bfloat16)


def attended_columns(att_ref):
    heads, blocks = att_ref.shape[:2]
    return jnp.concatenate(
        [
            jnp.concatenate([att_ref[head, block] for head in range(heads)], axis=0)
            for block in range(blocks)
        ],
        axis=1,
    )


def mixed_kernel(att_ref, wo_ref, mixed_ref):
    attended = attended_columns(att_ref).T
    mixed_ref[...] = dot(attended, wo_ref[...], ((1,), (0,))).astype(jnp.bfloat16)


def unpack_kernel(in_ref, gq_ref, gk_ref, gv_ref):
    blocks = in_ref.shape[1]
    low = lax.broadcasted_iota(jnp.int32, (BLOCK_ROWS, LANES), 1) < HEAD_WIDTH
    for block in range(blocks):
        rows = slice(block * BLOCK_ROWS, (block + 1) * BLOCK_ROWS)
        for head in range(0, HEADS, 2):
            columns = slice(head * HEAD_WIDTH, (head + 2) * HEAD_WIDTH)
            flat = jnp.concatenate([in_ref[head + i, block, :HEAD_WIDTH] for i in range(2)], axis=0)
            gq_ref[rows, columns] = flat.T
            one, two = (in_ref[head + i, block, HEAD_WIDTH:] for i in range(2))
            gk_ref[rows, columns] = jnp.concatenate(
                [one[:, :HEAD_WIDTH], two[:, :HEAD_WIDTH]], axis=1
            )
            gv_ref[rows, columns] = jnp.concatenate(
                [one[:, HEAD_WIDTH:], two[:, HEAD_WIDTH:]], axis=1
            )


def exchange(array):
    return lax.all_to_all(array, "seq", split_axis=0, concat_axis=0, tiled=True)


def local(queries, keys, values, upstream, w_out, key_blocks, block_counts):
    local_rows, width = queries.shape[1:]
    seq_size, dp_size = lax.axis_size("seq"), lax.axis_size("dp")
    lists, counts = key_blocks[0].T, block_counts[0]
    listed, blocks = lists.shape
    near_blocks = local_rows // BLOCK_ROWS
    up_rows = upstream[0]
    bf16, f32 = jnp.bfloat16, jnp.float32
    shape = jax.ShapeDtypeStruct
    smem, vmem = SMEM_SPEC, VMEM_SPEC

    packed, order = pack(counts, listed, queries[0], keys[0], values[0], up_rows, w_out)
    packed = exchange(packed)
    packed, up_rows = lax.optimization_barrier((packed, up_rows))
    half = width // 2
    core = (lax.axis_index("dp") % 2).reshape(1).astype(jnp.int32)
    other_core = [(i, i + 1 - 2 * (i % 2)) for i in range(dp_size)]
    own_up, send_up = call(
        split_columns_kernel,
        "split_columns",
        [shape((local_rows, half), bf16)] * 2,
        [smem, vmem],
        flops=10**8,
    )(core, up_rows)
    other_up = lax.ppermute(send_up, "dp", other_core)
    packed = packed.reshape(blocks, 2 * BLOCK_ROWS, LANES)
    listing = (lists, counts, order)
    turned = pltpu.VMEM((blocks, HEAD_WIDTH, BLOCK_ROWS), bf16)
    acc = (blocks, BLOCK_ROWS, LANES)
    half_turned = shape((blocks, HEAD_WIDTH, BLOCK_ROWS), bf16)

    attended, stats = call(
        forward_kernel,
        "forward",
        [half_turned, shape((blocks, 8, BLOCK_ROWS), f32)],
        [smem] * 3 + [vmem],
        [turned] + [pltpu.VMEM((listed * BLOCK_ROWS, BLOCK_ROWS), f32)] * FORWARD_TILE,
        flops=10 * 10**9,
    )(*listing, packed)

    attended = exchange(attended.reshape(seq_size, near_blocks, HEAD_WIDTH, BLOCK_ROWS))
    out_shape = (blocks, HEAD_WIDTH + BLOCK_ROWS, LANES)
    outgoing, token = call(
        functools.partial(backward_kernel, (0, FIRST_BLOCKS // FIRST_BACKWARD_TILE), True),
        "backward_first",
        [shape(out_shape, bf16), shape((8, LANES), f32)],
        [smem] * 3 + [vmem] * 2,
        [turned, pltpu.VMEM(acc, f32)],
        flops=10 * 10**9,
    )(*listing, packed, stats)

    attended, token = lax.optimization_barrier((attended, token))
    (chip_sum,) = call(
        weight_grad_kernel,
        "weight_grad",
        [shape((width, half), bf16)],
        [vmem] * 5,
        flops=10**9,
    )(attended, lax.ppermute(attended, "dp", other_core), own_up, other_up, token)

    chip_sum, stats = lax.optimization_barrier((chip_sum, stats))
    parts = exchange(chip_sum.reshape(seq_size, width // seq_size, half))
    outgoing, token = call(
        functools.partial(
            backward_kernel,
            (FIRST_BLOCKS // SECOND_BACKWARD_TILE, blocks // SECOND_BACKWARD_TILE),
            False,
        ),
        "backward_second",
        [shape(out_shape, bf16), shape((8, LANES), f32)],
        [smem] * 3 + [vmem] * 2 + [HBM_SPEC],
        [
            turned,
            pltpu.VMEM(acc, f32),
            pltpu.VMEM(out_shape, bf16),
            pltpu.SemaphoreType.DMA((1 + blocks // 4,)),
        ],
        flops=15 * 10**9,
        vmem=61,
        out_specs=[HBM_SPEC, vmem],
    )(*listing, packed, stats, outgoing)

    parts, _ = lax.optimization_barrier((parts, token))
    incoming = exchange(
        outgoing.reshape(seq_size, near_blocks, HEAD_WIDTH + BLOCK_ROWS, LANES)
    )
    grad_wo = jnp.sum(parts.astype(f32), axis=0)
    chips = dp_size // 2
    chip = lax.axis_index("dp") // 2
    apart = chips // 2
    while apart:
        below, above = jnp.split(grad_wo, 2, axis=1)
        upper = (chip // apart) % 2 == 1
        opposite = [(i, 2 * ((i // 2) ^ apart) + i % 2) for i in range(dp_size)]
        received = lax.ppermute(jnp.where(upper, below, above).astype(bf16), "dp", opposite)
        grad_wo = jnp.where(upper, above, below) + received.astype(f32)
        apart //= 2
    grad_wo = grad_wo * (1.0 / math.sqrt(dp_size * local_rows * seq_size))

    rows = shape((local_rows, width), bf16)
    (mixed,) = call(mixed_kernel, "mixed", [rows], [vmem] * 2, flops=10**9)(attended, w_out)
    gq, gk, gv = call(unpack_kernel, "unpack", [rows] * 3, [vmem])(incoming)
    full_shape = (1, local_rows, width)
    return (
        mixed.reshape(full_shape),
        gq.reshape(full_shape),
        gk.reshape(full_shape),
        gv.reshape(full_shape),
        grad_wo,
    )


def solution(mesh):
    nodes = P("dp", "seq", None)
    return jax.shard_map(
        local,
        mesh=mesh,
        in_specs=(nodes, nodes, nodes, nodes, P(), P("dp", None, None), P("dp", None)),
        out_specs=(nodes, nodes, nodes, nodes, P("seq", "dp")),
        check_vma=False,
    )
```
